32 devices in a mesh: rep: 2 (over x), node: 4 (over z), local: 4 (over y, core).
Axes of the slice: x: 2, y: 2, z: 4, core: 2. Of those that a mesh axis runs over, the one named last changes fastest.
Arguments:
- tokens: bfloat16 [2048, 7168], P(('rep', 'node', 'local')), parts along dimension 0, may hold values from -6 to 6
- expert_ids: int32 [2048, 2], P(('rep', 'node', 'local')), parts along dimension 0, may hold values from 0 to 7, as said below
- gate_values: bfloat16 [2048, 2], P(('rep', 'node', 'local')), parts along dimension 0, may hold values from 0.049804688 to 0.59765625
- w_gate: bfloat16 [16, 7168, 1024], P(('node', 'local')), may hold values from -0.0625 to 0.0625
- w_up: bfloat16 [16, 7168, 1024], P(('node', 'local')), may hold values from -0.0625 to 0.0625
- w_down: bfloat16 [16, 1024, 7168], P(('node', 'local')), may hold values from -0.125 to 0.125
Outputs:
- mixed: bfloat16 [2048, 7168], P(('rep', 'node', 'local')), parts along dimension 0
The draws below stay inside these ranges and needn't reach their ends.
There are 2 independent parts, one for each index of `rep`. The reference program is written for one: setup_inputs(seed, part) draws one part's arguments, and reference() takes and returns one part's arrays. A program takes and returns all parts, laid end to end along the dimension named above; an argument that names none is the same for every part. Nothing has to cross between parts.
Inputs may be any that keep to these rules, and one draw needn't show every extreme that they name: `expert_ids`: each token names 2 different experts (expert e lies on node e // 2): half of the tokens of one device name both experts of one node, the other half one expert on each of two different nodes. Among the 64 tokens of one device (aligned blocks of rows), exactly 24 reach each node.
All inputs are finite; a program needn't handle non-finite values.
Results may differ from the reference program's by a relative error of at most 0.008.
Values may be sent and summed in bfloat16 or wider, within the bound.
A program may use at most 192 MiB of HBM per device.

```python
import jax
import jax.numpy as jnp
from jax import lax

D = 7168
FF = 2048
TOK_DEV = 64
EXP_NODE = 2
TOP = 2
EXPERTS = 8
SPLIT = 2
BLOCK_FF = 1024
TOKENS = 1024
N_NODE = 4
N_LOCAL = 4


def draw_expert_ids(key, part):
    key = jax.random.fold_in(key, 11)
    blocks = N_NODE * N_LOCAL
    half = TOK_DEV // 2
    per_node = half // N_NODE

    def one_block(block_key):
        key_shift, key_bits, key_pair, key_order, key_swap = jax.random.split(block_key, 5)
        positions = jnp.arange(half, dtype=jnp.int32)
        first = positions // per_node
        rank = positions % per_node
        shifts = jax.random.randint(key_shift, (per_node,), 1, N_NODE)
        second = (first + shifts[rank]) % N_NODE
        bits = jax.random.randint(key_bits, (half, 2), 0, EXP_NODE)
        split_rows = jnp.stack([first * EXP_NODE + bits[:, 0], second * EXP_NODE + bits[:, 1]], axis=1)
        offset = jax.random.randint(key_pair, (half,), 0, 2)
        pair_rows = jnp.stack([first * EXP_NODE + offset, first * EXP_NODE + (1 - offset)], axis=1)
        named = jnp.concatenate([split_rows, pair_rows], axis=0)
        named = named[jax.random.permutation(key_order, TOK_DEV)]
        swap = jax.random.randint(key_swap, (TOK_DEV, 1), 0, 2)
        return jnp.where(swap == 1, named[:, ::-1], named)
    block_keys = jax.random.split(key, blocks)
    return jax.vmap(one_block)(block_keys).reshape(blocks * TOK_DEV, TOP).astype(jnp.int32)


def level_of(own_key, extent, shards, low, largest):
    def one(axis_at, shards_of):
        steps = jax.random.uniform(jax.random.fold_in(jax.random.fold_in(own_key, 6), axis_at), (shards_of,), jnp.float32, low / len(shards), largest / len(shards))
        return jnp.repeat(jnp.exp(steps), extent[axis_at] // shards_of).reshape((-1,) + (1,) * (len(extent) - axis_at - 1))

    loudness = one(*shards[0])
    for cut in shards[1:]:
        loudness = loudness * one(*cut)
    return loudness


def gaussian(own_key, dims, width, most, cuts=(), held_as=jnp.bfloat16):
    array = jax.random.normal(own_key, dims, jnp.float32) * width
    if len(cuts) > 0:
        array = level_of(own_key, dims, cuts, -0.22, 0.18) * array
    return jnp.clip(array, min=-most, max=most).astype(held_as)


def setup_inputs(seed: int = 0, part: int = 0) -> dict:
    key_of = jax.random.split(jax.random.key(seed), 7)
    part_splits = jax.random.split(jax.random.fold_in(key_of[6], part), 7)
    return {
        "tokens": gaussian(part_splits[0], (TOKENS, D), 1.0, 6.0, ((0, 16),)),
        "expert_ids": draw_expert_ids(jax.random.fold_in(jax.random.fold_in(key_of[6], part), 71), part),
        "gate_values": jnp.clip(0.049804688 + 0.54785156 * jax.random.uniform(part_splits[2], (TOKENS, TOP), jnp.float32) ** level_of(part_splits[2], (TOKENS, TOP), ((0, 16),), -0.2, 0.2), 0.049804688, 0.59765625).astype(jnp.bfloat16),
        "w_gate": gaussian(key_of[3], (EXPERTS * SPLIT, D, BLOCK_FF), D ** -0.5, 0.0625, ((0, 16),)),
        "w_up": gaussian(key_of[4], (EXPERTS * SPLIT, D, BLOCK_FF), D ** -0.5, 0.0625, ((0, 16),)),
        "w_down": gaussian(key_of[5], (EXPERTS * SPLIT, BLOCK_FF, D), FF ** -0.5, 0.125, ((0, 16),)),
    }


def reference(tokens, expert_ids, gate_values, w_gate, w_up, w_down):
    experts = EXP_NODE * N_NODE
    split = N_LOCAL // EXP_NODE
    labels = jnp.arange(experts, dtype=jnp.int32)
    matches = expert_ids[:, :, None] == labels[None, None, :]
    gate_table = jnp.sum(jnp.where(matches, gate_values.astype(jnp.float32)[:, :, None], jnp.float32(0.0)), axis=1)
    owner = expert_ids // EXP_NODE
    count = 3 * tokens.shape[0] // (2 * N_NODE)

    def node_step(node, summed):
        node = jnp.asarray(node).astype(jnp.int32)
        reached = jnp.any(owner == node, axis=1)
        order = jnp.argsort(jnp.where(reached, 0, 1).astype(jnp.int32), stable=True)[:count].astype(jnp.int32)
        rows = tokens[order]
        gates = gate_table[order]

        def block_step(accum, lane):
            index = (node * N_LOCAL + lane).astype(jnp.int32)
            expert = (node * EXP_NODE + lane // split).astype(jnp.int32)
            gate_w = lax.dynamic_index_in_dim(w_gate, index, 0, False)
            up_w = lax.dynamic_index_in_dim(w_up, index, 0, False)
            down_w = lax.dynamic_index_in_dim(w_down, index, 0, False)
            weight = lax.dynamic_slice_in_dim(gates, expert, 1, 1)
            gate = jnp.dot(rows, gate_w, preferred_element_type=jnp.float32)
            upper = jnp.dot(rows, up_w, preferred_element_type=jnp.float32)
            gated = (weight * jax.nn.silu(gate) * upper).astype(jnp.bfloat16)
            piece = lax.optimization_barrier(jnp.dot(gated, down_w, preferred_element_type=jnp.float32).astype(jnp.bfloat16))
            return accum + piece.astype(jnp.float32), None

        node_sum, _ = lax.scan(block_step, jnp.zeros((count, tokens.shape[1]), jnp.float32), jnp.arange(N_LOCAL, dtype=jnp.int32))
        node_out = lax.optimization_barrier(node_sum.astype(jnp.bfloat16))
        return summed.at[order].add(node_out.astype(jnp.float32))

    summed = lax.fori_loop(0, N_NODE, node_step, jnp.zeros(tokens.shape, jnp.float32))
    return summed.astype(jnp.bfloat16)
```

```python
import functools

import jax
import jax.numpy as jnp
from jax import lax
from jax.experimental import pallas as pl
from jax.experimental.pallas import tpu as pltpu
from jax.sharding import PartitionSpec as P

EXP_NODE = 2
MESH = pl.DeviceIdType.MESH
F32 = jnp.float32
BF16 = jnp.bfloat16
LANES = 128
GATE_TILE = 256
TILE = 512
NT = (((1,), (1,)), ((), ()))

TOK, TBL, OUT, Z, Y, C1, C2, RC, RY, RZ = 0, 1, 2, 4, 8, 12, 16, 20, 24, 28
SEMS = 32


def fused_kernel(
    cap,
    tokens,
    ids_t,
    gates_t,
    w_gate,
    w_up,
    w_down,
    out,
    wg,
    wu,
    wd,
    x,
    sendz,
    tok_n,
    tbl,
    rows_before,
    rows_reached,
    sel,
    hid,
    crecv,
    yrecv,
    zret,
    load_sem,
    send_sem,
    recv_sem,
):
    half = tokens.shape[1] // 2
    count_tok = tokens.shape[0]
    pair = 2 * cap
    ff = wg.shape[1]
    me = lax.axis_index("node")
    lane = lax.axis_index("local")
    y = lane // 2
    c = lane % 2
    core_nbr = {"local": lane + 1 - 2 * c}
    y_nbr = {"local": (lane + 2) % 4}
    node_of = [me, me + 1 - 2 * (me % 2), (me + 2) % 4, 3 - me]

    loads = [
        pltpu.make_async_copy(src.at[0], dst, load_sem.at[i])
        for i, (src, dst) in enumerate(((w_gate, wg), (w_up, wu), (w_down, wd)))
    ]
    barrier = pltpu.get_barrier_semaphore()
    partners = [core_nbr, y_nbr] + [{"node": node_of[k]} for k in (1, 2, 3)]
    for partner in partners:
        pl.semaphore_signal(barrier, inc=1, device_id=partner, device_id_type=MESH)
    pl.semaphore_wait(barrier, len(partners))

    def remote(src, dst, number, device):
        return pltpu.make_async_remote_copy(
            src_ref=src,
            dst_ref=dst,
            send_sem=send_sem.at[number],
            recv_sem=recv_sem.at[number],
            device_id=device,
            device_id_type=MESH,
        )

    own_at = pl.multiple_of(c * half, LANES)
    nbr_at = pl.multiple_of((1 - c) * half, LANES)
    tok_copy = remote(tokens.at[:, pl.ds(nbr_at, half)], tok_n, TOK, core_nbr)
    tok_copy.start()
    row = lax.broadcasted_iota(jnp.int32, (LANES, count_tok), 0)
    tbl[0] = jnp.where(ids_t[0:1, :] == row, gates_t[0:1, :], 0.0) + jnp.where(
        ids_t[1:2, :] == row, gates_t[1:2, :], 0.0
    )
    tbl_copy = remote(tbl.at[0], tbl.at[1], TBL, core_nbr)
    tbl_copy.start()

    def select(which, first):
        named = jnp.where(tbl[which] != 0.0, 1.0, 0.0).astype(BF16)
        pool = jnp.where(
            lax.broadcasted_iota(jnp.int32, (8, LANES), 1) // EXP_NODE
            == lax.broadcasted_iota(jnp.int32, (8, LANES), 0),
            1.0,
            0.0,
        ).astype(BF16)
        reached = jnp.minimum(jnp.dot(pool, named, preferred_element_type=F32), 1.0)
        upper = jnp.where(
            lax.broadcasted_iota(jnp.int32, (count_tok, count_tok), 0)
            < lax.broadcasted_iota(jnp.int32, (count_tok, count_tok), 1),
            1.0,
            0.0,
        ).astype(BF16)
        rows_before[...] = jnp.dot(reached.astype(BF16), upper, preferred_element_type=F32)
        rows_reached[...] = reached
        slot = lax.broadcasted_iota(jnp.int32, (pair, count_tok), 0)
        for k in range(4):
            before = rows_before[pl.ds(node_of[k], 1), :].astype(jnp.int32) + first
            there = rows_reached[pl.ds(node_of[k], 1), :]
            sel[which, k * pair : (k + 1) * pair, :] = jnp.where(
                before == slot, there, 0.0
            ).astype(BF16)

    select(0, cap * c)
    tbl_copy.wait_recv()
    select(1, cap * (1 - c))
    tok_copy.wait_recv()

    def build(k, dst):
        s_own = sel[0, k * pair : (k + 1) * pair, :]
        s_nbr = sel[1, k * pair : (k + 1) * pair, :]
        gates = lax.dot_general(
            s_own, tbl[0].astype(BF16), NT, preferred_element_type=F32
        ) + lax.dot_general(s_nbr, tbl[1].astype(BF16), NT, preferred_element_type=F32)
        dst[:, half : half + LANES] = gates.astype(BF16)

        @pl.loop(0, half // TILE)
        def _(j):
            at = pl.multiple_of(j * TILE, TILE)
            here = pl.multiple_of(own_at + at, LANES)
            got = jnp.dot(s_own, tokens[:, pl.ds(here, TILE)], preferred_element_type=F32)
            got += jnp.dot(s_nbr, tok_n[:, pl.ds(at, TILE)], preferred_element_type=F32)
            dst[:, pl.ds(at, TILE)] = got.astype(BF16)

    def z_copy(k):
        return remote(
            sendz.at[k - 1], x.at[c, me, y], Z + k, {"node": node_of[k]}
        )

    def y_copy(k):
        here = x.at[c, node_of[k], y]
        return remote(here, here, Y + k, y_nbr)

    def c1_copy(k):
        here = x.at[c, node_of[k], y]
        return remote(here, here, C1 + k, core_nbr)

    def c2_copy(k):
        here = x.at[c, node_of[k], 1 - y]
        return remote(here, here, C2 + k, core_nbr)

    def rc_copy(k):
        return remote(
            x.at[1 - c, node_of[k], :, :, pl.ds(0, half)], crecv.at[k], RC + k, core_nbr
        )

    def ry_copy(k):
        return remote(crecv.at[k, 1 - y], yrecv.at[k], RY + k, y_nbr)

    def rz_copy(k):
        return remote(crecv.at[k, y], zret.at[k], RZ + k, {"node": node_of[k]})

    def take_z(k):
        if k > 0:
            z_copy(k).wait_recv()
        y_copy(k).start()
        c1_copy(k).start()

    def take_y(k):
        y_copy(k).wait_recv()
        c2_copy(k).start()

    def compute(k):
        m = node_of[k]
        c1_copy(k).wait()
        c2_copy(k).wait()
        y_copy(k).wait_send()
        count = 2 * pair
        table = x[c, m, :, :, half : half + LANES].reshape(count, LANES).astype(F32)
        mine = lax.broadcasted_iota(jnp.int32, (count, LANES), 1) == me * EXP_NODE + y
        weight = jnp.sum(jnp.where(mine, table, 0.0), axis=1, keepdims=True)

        @pl.loop(0, ff // GATE_TILE)
        def _(j):
            cols = pl.ds(pl.multiple_of(j * GATE_TILE, GATE_TILE), GATE_TILE)
            x0 = x[0, m, :, :, :half].reshape(count, half)
            x1 = x[1, m, :, :, :half].reshape(count, half)
            gate = jnp.dot(x0, wg[:half, cols], preferred_element_type=F32)
            gate += jnp.dot(x1, wg[half:, cols], preferred_element_type=F32)
            upper = jnp.dot(x0, wu[:half, cols], preferred_element_type=F32)
            upper += jnp.dot(x1, wu[half:, cols], preferred_element_type=F32)
            hid[:, cols] = (weight * (gate / (1.0 + jnp.exp(-gate))) * upper).astype(BF16)

        for h in range(2):

            @pl.loop(0, half // TILE)
            def _(j):
                at = pl.multiple_of(j * TILE, TILE)
                part = jnp.dot(
                    hid[...], wd[:, pl.ds(pl.multiple_of(h * half + at, TILE), TILE)],
                    preferred_element_type=F32,
                )
                x[h, m, :, :, pl.ds(at, TILE)] = part.astype(BF16).reshape(2, pair, TILE)

        rc_copy(k).start()

    def fold_core(k):
        rc_copy(k).wait_recv()
        crecv[k, 1 - y] = (
            crecv[k, 1 - y].astype(F32) + x[c, node_of[k], 1 - y, :, :half].astype(F32)
        ).astype(BF16)
        ry_copy(k).start()

    def fold_y(k):
        ry_copy(k).wait_recv()
        total = (
            crecv[k, y].astype(F32)
            + x[c, node_of[k], y, :, :half].astype(F32)
            + yrecv[k].astype(F32)
        ).astype(BF16)
        if k == 0:
            zret[0] = total
        else:
            crecv[k, y] = total
            rz_copy(k).start()

    build(2, sendz.at[1])
    z_copy(2).start()
    build(1, sendz.at[0])
    z_copy(1).start()
    build(0, x.at[c, me, y])
    take_z(0)
    for load in loads:
        load.start()
    build(3, sendz.at[2])
    take_y(0)
    z_copy(2).wait_send()
    z_copy(3).start()
    take_z(1)
    take_z(2)
    for load in loads:
        load.wait()
    compute(0)
    take_y(1)
    take_y(2)
    fold_core(0)
    compute(1)
    take_z(3)
    fold_core(1)
    fold_y(0)
    compute(2)
    take_y(3)
    fold_core(2)
    fold_y(1)
    compute(3)
    fold_y(2)
    fold_core(3)
    fold_y(3)

    eye = jnp.where(
        lax.broadcasted_iota(jnp.int32, (count_tok, count_tok), 0)
        == lax.broadcasted_iota(jnp.int32, (count_tok, count_tok), 1),
        1.0,
        0.0,
    ).astype(BF16)
    for k in (1, 2, 3):
        rz_copy(k).wait_recv()
    out_copy = remote(
        tok_n, out.at[:, pl.ds(own_at, half)], OUT, core_nbr
    )
    for which in (1, 0):
        back = lax.dot_general(eye, sel[which], NT, preferred_element_type=F32).astype(BF16)

        @pl.loop(0, half // TILE)
        def _(j):
            at = pl.multiple_of(j * TILE, TILE)
            got = zret[:, :, pl.ds(at, TILE)].reshape(4 * pair, TILE)
            mixed = jnp.dot(back, got, preferred_element_type=F32).astype(BF16)
            if which == 1:
                tok_n[:, pl.ds(at, TILE)] = mixed
            else:
                out[:, pl.ds(pl.multiple_of(own_at + at, LANES), TILE)] = mixed

        if which == 1:
            out_copy.start()
    out_copy.wait()
    tok_copy.wait_send()
    tbl_copy.wait_send()
    z_copy(1).wait_send()
    z_copy(3).wait_send()
    for k in range(4):
        rc_copy(k).wait_send()
        ry_copy(k).wait_send()
        if k > 0:
            rz_copy(k).wait_send()


def fused(tokens, expert_ids, gate_values, w_gate, w_up, w_down):
    count_tok, width = tokens.shape
    nodes = lax.axis_size("node")
    cap = 3 * count_tok // (2 * nodes)
    pair = 2 * cap
    half = width // 2
    ff = w_gate.shape[2]
    vmem = pl.BlockSpec(memory_space=pltpu.VMEM)
    hbm = pl.BlockSpec(memory_space=pl.ANY)
    dma = pltpu.SemaphoreType.DMA
    return pl.pallas_call(
        functools.partial(fused_kernel, cap),
        out_shape=jax.ShapeDtypeStruct((count_tok, width), BF16),
        in_specs=[vmem, vmem, vmem, hbm, hbm, hbm],
        out_specs=vmem,
        scratch_shapes=[
            pltpu.VMEM((width, ff), BF16),
            pltpu.VMEM((width, ff), BF16),
            pltpu.VMEM((ff, width), BF16),
            pltpu.VMEM((2, nodes, 2, pair, half + LANES), BF16),
            pltpu.VMEM((nodes - 1, pair, half + LANES), BF16),
            pltpu.VMEM((count_tok, half), BF16),
            pltpu.VMEM((2, LANES, count_tok), F32),
            pltpu.VMEM((8, count_tok), F32),
            pltpu.VMEM((8, count_tok), F32),
            pltpu.VMEM((2, nodes * pair, count_tok), BF16),
            pltpu.VMEM((2 * pair, ff), BF16),
            pltpu.VMEM((nodes, 2, pair, half), BF16),
            pltpu.VMEM((nodes, pair, half), BF16),
            pltpu.VMEM((nodes, pair, half), BF16),
            dma((3,)),
            dma((SEMS,)),
            dma((SEMS,)),
        ],
        compiler_params=pltpu.CompilerParams(
            collective_id=0, has_side_effects=True, vmem_limit_bytes=61 * 1024 * 1024
        ),
        cost_estimate=pl.CostEstimate(
            flops=12 * nodes * pair * width * ff,
            bytes_accessed=6 * width * ff,
            transcendentals=2 * nodes * pair * ff,
        ),
    )(
        tokens,
        expert_ids.T,
        gate_values.astype(F32).T,
        w_gate,
        w_up,
        w_down,
    )


def local(tokens, expert_ids, gate_values, w_gate, w_up, w_down):
    nodes = lax.axis_size("node")
    lanes = lax.axis_size("local")
    split = lanes // EXP_NODE
    width = tokens.shape[1]
    count_tok = tokens.shape[0]
    capacity = 3 * count_tok // (2 * nodes)
    node_labels = jnp.arange(nodes, dtype=jnp.int32)
    owner = expert_ids // EXP_NODE
    reached = jnp.any(owner[:, :, None] == node_labels[None, None, :], axis=1).astype(jnp.int32)
    before = jnp.cumsum(reached, axis=0) - reached
    slot_labels = jnp.arange(capacity, dtype=jnp.int32)
    picked = (before.T[:, None, :] == slot_labels[None, :, None]) & (reached.T[:, None, :] == 1)
    selection = picked.reshape(nodes * capacity, count_tok).astype(jnp.bfloat16)
    send_rows = (
        jnp.dot(selection, tokens, preferred_element_type=jnp.float32)
        .astype(jnp.bfloat16)
        .reshape(nodes, capacity, width)
    )
    expert_labels = jnp.arange(nodes * EXP_NODE, dtype=jnp.int32)
    matches = expert_ids[:, :, None] == expert_labels[None, None, :]
    gate_table = jnp.sum(
        jnp.where(matches, gate_values.astype(jnp.float32)[:, :, None], jnp.float32(0.0)), axis=1
    )
    gate_table = gate_table.reshape(count_tok, nodes, EXP_NODE)
    slot_gates = jnp.einsum("mct,tmk->mck", picked.astype(jnp.float32), gate_table).astype(
        jnp.bfloat16
    )
    arrived, arrived_gates = (
        lax.all_to_all(send_rows, "node", split_axis=0, concat_axis=0, tiled=True),
        lax.all_to_all(slot_gates, "node", split_axis=0, concat_axis=0, tiled=True),
    )
    gathered, gathered_gates = (
        lax.all_gather(arrived, "local", axis=0, tiled=True),
        lax.all_gather(arrived_gates, "local", axis=0, tiled=True),
    )
    rows_all = gathered.reshape(-1, width)
    gates_all = gathered_gates.reshape(-1, EXP_NODE)
    which = lax.axis_index("local") // split
    own_gate = lax.dynamic_slice_in_dim(gates_all, which, 1, 1).astype(jnp.float32)
    gate = jnp.dot(rows_all, w_gate[0], preferred_element_type=jnp.float32)
    upper = jnp.dot(rows_all, w_up[0], preferred_element_type=jnp.float32)
    gated = (own_gate * jax.nn.silu(gate) * upper).astype(jnp.bfloat16)
    down_w = w_down[0]
    own_rows = lax.psum_scatter(
        jnp.dot(gated, down_w, preferred_element_type=jnp.float32).astype(jnp.bfloat16),
        "local",
        scatter_dimension=0,
        tiled=True,
    )
    returned = lax.all_to_all(
        own_rows.reshape(nodes, capacity, width), "node", split_axis=0, concat_axis=0, tiled=True
    )
    mixed = jnp.dot(
        selection.T, returned.reshape(nodes * capacity, width), preferred_element_type=jnp.float32
    )
    return mixed.astype(jnp.bfloat16)


def solution(mesh):
    placed = (
        P(("rep", "node", "local"), None),
        P(("rep", "node", "local"), None),
        P(("rep", "node", "local"), None),
        P(("node", "local"), None, None),
        P(("node", "local"), None, None),
        P(("node", "local"), None, None),
    )
    paired = mesh.shape["node"] == 4 and mesh.shape["local"] == 4
    return jax.shard_map(
        fused if paired else local,
        mesh=mesh,
        in_specs=placed,
        out_specs=P(("rep", "node", "local"), None),
        check_vma=False,
    )
```

```python
import functools

import jax
import jax.numpy as jnp
from jax import lax
from jax.experimental import pallas as pl
from jax.experimental.pallas import tpu as pltpu
from jax.sharding import PartitionSpec as P

EXP_NODE = 2
MESH = pl.DeviceIdType.MESH
F32 = jnp.float32
BF16 = jnp.bfloat16
LANES = 128
GATE_TILE = 256
TILE = 512
NT = (((1,), (1,)), ((), ()))

TOK, TBL, OUT, Z, Y, C1, C2, RC, RY, RZ = 0, 1, 2, 4, 12, 20, 24, 28, 32, 40
SEMS = 48
SLOT = (1, 3, 2, 0)


def fused_kernel(
    cap,
    tokens,
    ids_t,
    gates_t,
    w_gate,
    w_up,
    w_down,
    out,
    wg,
    wu,
    wd,
    x,
    sendz,
    tok_n,
    tbl,
    rows_before,
    rows_reached,
    sel,
    hid,
    crecv,
    yrecv,
    zret,
    load_sem,
    send_sem,
    recv_sem,
):
    half = tokens.shape[1] // 2
    count_tok = tokens.shape[0]
    pair = 2 * cap
    ff = wg.shape[1]
    me = lax.axis_index("node")
    lane = lax.axis_index("local")
    y = lane // 2
    c = lane % 2
    core_nbr = {"local": lane + 1 - 2 * c}
    y_nbr = {"local": (lane + 2) % 4}
    node_of = [me, me + 1 - 2 * (me % 2), (me + 2) % 4, 3 - me]

    loads = [
        pltpu.make_async_copy(src.at[0], dst, load_sem.at[i])
        for i, (src, dst) in enumerate(((w_gate, wg), (w_up, wu), (w_down, wd)))
    ]
    barrier = pltpu.get_barrier_semaphore()
    partners = [core_nbr, y_nbr] + [{"node": node_of[k]} for k in (1, 2, 3)]
    for partner in partners:
        pl.semaphore_signal(barrier, inc=1, device_id=partner, device_id_type=MESH)
    pl.semaphore_wait(barrier, len(partners))

    def remote(src, dst, number, device):
        return pltpu.make_async_remote_copy(
            src_ref=src,
            dst_ref=dst,
            send_sem=send_sem.at[number],
            recv_sem=recv_sem.at[number],
            device_id=device,
            device_id_type=MESH,
        )

    own_at = pl.multiple_of(c * half, LANES)
    nbr_at = pl.multiple_of((1 - c) * half, LANES)
    tok_copy = remote(tokens.at[:, pl.ds(nbr_at, half)], tok_n, TOK, core_nbr)
    tok_copy.start()
    row = lax.broadcasted_iota(jnp.int32, (LANES, count_tok), 0)
    tbl[0] = jnp.where(ids_t[0:1, :] == row, gates_t[0:1, :], 0.0) + jnp.where(
        ids_t[1:2, :] == row, gates_t[1:2, :], 0.0
    )
    tbl_copy = remote(tbl.at[0], tbl.at[1], TBL, core_nbr)
    tbl_copy.start()

    def select(which, first):
        named = jnp.where(tbl[which] != 0.0, 1.0, 0.0).astype(BF16)
        pool = jnp.where(
            lax.broadcasted_iota(jnp.int32, (8, LANES), 1) // EXP_NODE
            == lax.broadcasted_iota(jnp.int32, (8, LANES), 0),
            1.0,
            0.0,
        ).astype(BF16)
        reached = jnp.minimum(jnp.dot(pool, named, preferred_element_type=F32), 1.0)
        upper = jnp.where(
            lax.broadcasted_iota(jnp.int32, (count_tok, count_tok), 0)
            < lax.broadcasted_iota(jnp.int32, (count_tok, count_tok), 1),
            1.0,
            0.0,
        ).astype(BF16)
        rows_before[...] = jnp.dot(reached.astype(BF16), upper, preferred_element_type=F32)
        rows_reached[...] = reached
        slot = lax.broadcasted_iota(jnp.int32, (pair, count_tok), 0)
        for k in range(4):
            before = rows_before[pl.ds(node_of[k], 1), :].astype(jnp.int32) + first
            there = rows_reached[pl.ds(node_of[k], 1), :]
            sel[which, k * pair : (k + 1) * pair, :] = jnp.where(
                before == slot, there, 0.0
            ).astype(BF16)

    select(0, cap * c)
    tbl_copy.wait_recv()
    select(1, cap * (1 - c))
    tok_copy.wait_recv()

    def build(k, dst):
        s_own = sel[0, k * pair : (k + 1) * pair, :]
        s_nbr = sel[1, k * pair : (k + 1) * pair, :]
        gates = lax.dot_general(
            s_own, tbl[0].astype(BF16), NT, preferred_element_type=F32
        ) + lax.dot_general(s_nbr, tbl[1].astype(BF16), NT, preferred_element_type=F32)
        dst[:, half : half + LANES] = gates.astype(BF16)

        @pl.loop(0, half // TILE)
        def _(j):
            at = pl.multiple_of(j * TILE, TILE)
            here = pl.multiple_of(own_at + at, LANES)
            got = jnp.dot(s_own, tokens[:, pl.ds(here, TILE)], preferred_element_type=F32)
            got += jnp.dot(s_nbr, tok_n[:, pl.ds(at, TILE)], preferred_element_type=F32)
            dst[:, pl.ds(at, TILE)] = got.astype(BF16)

    cut = half // 2
    going = (pl.ds(0, cut), pl.ds(cut, half - cut + LANES))
    coming = (pl.ds(0, cut), pl.ds(cut, half - cut))

    def z_copy(k, p):
        return remote(
            sendz.at[k - 1, :, going[p]],
            x.at[c, SLOT[k], y, :, going[p]],
            Z + 2 * k + p,
            {"node": node_of[k]},
        )

    def y_copy(k, p):
        here = x.at[c, SLOT[k], y, :, going[p]]
        return remote(here, here, Y + 2 * k + p, y_nbr)

    def c1_copy(k):
        here = x.at[c, SLOT[k], y]
        return remote(here, here, C1 + k, core_nbr)

    def c2_copy(k):
        here = x.at[c, SLOT[k], 1 - y]
        return remote(here, here, C2 + k, core_nbr)

    def rc_copy(k):
        return remote(
            x.at[1 - c, SLOT[k], :, :, pl.ds(0, half)], crecv.at[k], RC + k, core_nbr
        )

    def ry_copy(k, p):
        return remote(
            crecv.at[k, 1 - y, :, coming[p]], yrecv.at[k, :, coming[p]], RY + 2 * k + p, y_nbr
        )

    def rz_copy(k, p):
        return remote(
            crecv.at[k, y, :, coming[p]],
            zret.at[k, :, coming[p]],
            RZ + 2 * k + p,
            {"node": node_of[k]},
        )

    def take_z(k, p):
        if k > 0:
            z_copy(k, p).wait_recv()
        y_copy(k, p).start()
        if p == 1:
            c1_copy(k).start()

    def take_y(k):
        for p in range(2):
            y_copy(k, p).wait_recv()
        c2_copy(k).start()

    count = 2 * 2 * pair

    def up(rounds):
        first = SLOT[rounds[0]]
        both = pl.ds(first, 2)
        for k in rounds:
            c1_copy(k).wait_recv()
            c2_copy(k).wait_recv()
        table = x[c, both, :, :, half : half + LANES].reshape(count, LANES).astype(F32)
        mine = lax.broadcasted_iota(jnp.int32, (count, LANES), 1) == me * EXP_NODE + y
        weight = jnp.sum(jnp.where(mine, table, 0.0), axis=1, keepdims=True)

        @pl.loop(0, ff // GATE_TILE)
        def _(j):
            cols = pl.ds(pl.multiple_of(j * GATE_TILE, GATE_TILE), GATE_TILE)
            x0 = x[0, both, :, :, :half].reshape(count, half)
            x1 = x[1, both, :, :, :half].reshape(count, half)
            gate = jnp.dot(x0, wg[:half, cols], preferred_element_type=F32)
            gate += jnp.dot(x1, wg[half:, cols], preferred_element_type=F32)
            upper = jnp.dot(x0, wu[:half, cols], preferred_element_type=F32)
            upper += jnp.dot(x1, wu[half:, cols], preferred_element_type=F32)
            hid[:, cols] = (weight * (gate / (1.0 + jnp.exp(-gate))) * upper).astype(BF16)

    def down(rounds, h):
        both = pl.ds(SLOT[rounds[0]], 2)

        @pl.loop(0, half // TILE)
        def _(j):
            at = pl.multiple_of(j * TILE, TILE)
            part = jnp.dot(
                hid[...],
                wd[:, pl.ds(pl.multiple_of(h * half + at, TILE), TILE)],
                preferred_element_type=F32,
            )
            x[h, both, :, :, pl.ds(at, TILE)] = part.astype(BF16).reshape(2, 2, pair, TILE)

    def down_nbr(rounds):
        down(rounds, 1 - c)
        for k in rounds:
            rc_copy(k).start()

    def down_own(rounds):
        for k in rounds:
            c1_copy(k).wait_send()
            c2_copy(k).wait_send()
            for p in range(2):
                y_copy(k, p).wait_send()
        down(rounds, c)

    def fold_core(k):
        rc_copy(k).wait_recv()
        for p in range(2):
            cols = coming[p]
            crecv[k, 1 - y, :, cols] = (
                crecv[k, 1 - y, :, cols].astype(F32)
                + x[c, SLOT[k], 1 - y, :, cols].astype(F32)
            ).astype(BF16)
            ry_copy(k, p).start()

    def fold_y(k):
        for p in range(2):
            cols = coming[p]
            ry_copy(k, p).wait_recv()
            total = (
                crecv[k, y, :, cols].astype(F32)
                + x[c, SLOT[k], y, :, cols].astype(F32)
                + yrecv[k, :, cols].astype(F32)
            ).astype(BF16)
            if k == 0:
                zret[0, :, cols] = total
            else:
                crecv[k, y, :, cols] = total
                rz_copy(k, p).start()

    build(3, sendz.at[2])
    z_copy(3, 0).start()
    z_copy(3, 1).start()
    build(0, x.at[c, SLOT[0], y])
    take_z(0, 0)
    take_z(0, 1)
    for load in loads:
        load.start()
    build(2, sendz.at[1])
    build(1, sendz.at[0])
    take_z(3, 0)
    z_copy(3, 0).wait_send()
    z_copy(2, 0).start()
    take_y(0)
    take_z(3, 1)
    z_copy(3, 1).wait_send()
    z_copy(2, 1).start()
    z_copy(1, 0).start()
    z_copy(1, 1).start()
    take_y(3)
    for load in loads:
        load.wait()
    up((3, 0))
    take_z(2, 0)
    down_nbr((3, 0))
    take_z(2, 1)
    down_own((3, 0))
    fold_core(3)
    take_z(1, 0)
    take_z(1, 1)
    fold_y(3)
    take_y(2)
    take_y(1)
    up((2, 1))
    fold_core(0)
    down_nbr((2, 1))
    down_own((2, 1))
    fold_core(2)
    fold_core(1)
    fold_y(0)
    fold_y(2)
    fold_y(1)

    eye = jnp.where(
        lax.broadcasted_iota(jnp.int32, (count_tok, count_tok), 0)
        == lax.broadcasted_iota(jnp.int32, (count_tok, count_tok), 1),
        1.0,
        0.0,
    ).astype(BF16)
    for k in (1, 2, 3):
        for p in range(2):
            rz_copy(k, p).wait_recv()
    out_copy = remote(
        tok_n, out.at[:, pl.ds(own_at, half)], OUT, core_nbr
    )
    for which in (1, 0):
        back = lax.dot_general(eye, sel[which], NT, preferred_element_type=F32).astype(BF16)

        @pl.loop(0, half // TILE)
        def _(j):
            at = pl.multiple_of(j * TILE, TILE)
            got = zret[:, :, pl.ds(at, TILE)].reshape(4 * pair, TILE)
            mixed = jnp.dot(back, got, preferred_element_type=F32).astype(BF16)
            if which == 1:
                tok_n[:, pl.ds(at, TILE)] = mixed
            else:
                out[:, pl.ds(pl.multiple_of(own_at + at, LANES), TILE)] = mixed

        if which == 1:
            out_copy.start()
    out_copy.wait()
    tok_copy.wait_send()
    tbl_copy.wait_send()
    for p in range(2):
        z_copy(1, p).wait_send()
        z_copy(2, p).wait_send()
    for k in range(4):
        rc_copy(k).wait_send()
        for p in range(2):
            ry_copy(k, p).wait_send()
            if k > 0:
                rz_copy(k, p).wait_send()


def fused(tokens, expert_ids, gate_values, w_gate, w_up, w_down):
    count_tok, width = tokens.shape
    nodes = lax.axis_size("node")
    cap = 3 * count_tok // (2 * nodes)
    pair = 2 * cap
    half = width // 2
    ff = w_gate.shape[2]
    vmem = pl.BlockSpec(memory_space=pltpu.VMEM)
    hbm = pl.BlockSpec(memory_space=pl.ANY)
    dma = pltpu.SemaphoreType.DMA
    return pl.pallas_call(
        functools.partial(fused_kernel, cap),
        out_shape=jax.ShapeDtypeStruct((count_tok, width), BF16),
        in_specs=[vmem, vmem, vmem, hbm, hbm, hbm],
        out_specs=vmem,
        scratch_shapes=[
            pltpu.VMEM((width, ff), BF16),
            pltpu.VMEM((width, ff), BF16),
            pltpu.VMEM((ff, width), BF16),
            pltpu.VMEM((2, nodes, 2, pair, half + LANES), BF16),
            pltpu.VMEM((nodes - 1, pair, half + LANES), BF16),
            pltpu.VMEM((count_tok, half), BF16),
            pltpu.VMEM((2, LANES, count_tok), F32),
            pltpu.VMEM((8, count_tok), F32),
            pltpu.VMEM((8, count_tok), F32),
            pltpu.VMEM((2, nodes * pair, count_tok), BF16),
            pltpu.VMEM((4 * pair, ff), BF16),
            pltpu.VMEM((nodes, 2, pair, half), BF16),
            pltpu.VMEM((nodes, pair, half), BF16),
            pltpu.VMEM((nodes, pair, half), BF16),
            dma((3,)),
            dma((SEMS,)),
            dma((SEMS,)),
        ],
        compiler_params=pltpu.CompilerParams(
            collective_id=0, has_side_effects=True, vmem_limit_bytes=61 * 1024 * 1024
        ),
        cost_estimate=pl.CostEstimate(
            flops=12 * nodes * pair * width * ff,
            bytes_accessed=6 * width * ff,
            transcendentals=2 * nodes * pair * ff,
        ),
    )(
        tokens,
        expert_ids.T,
        gate_values.astype(F32).T,
        w_gate,
        w_up,
        w_down,
    )


def local(tokens, expert_ids, gate_values, w_gate, w_up, w_down):
    nodes = lax.axis_size("node")
    lanes = lax.axis_size("local")
    split = lanes // EXP_NODE
    width = tokens.shape[1]
    count_tok = tokens.shape[0]
    capacity = 3 * count_tok // (2 * nodes)
    node_labels = jnp.arange(nodes, dtype=jnp.int32)
    owner = expert_ids // EXP_NODE
    reached = jnp.any(owner[:, :, None] == node_labels[None, None, :], axis=1).astype(jnp.int32)
    before = jnp.cumsum(reached, axis=0) - reached
    slot_labels = jnp.arange(capacity, dtype=jnp.int32)
    picked = (before.T[:, None, :] == slot_labels[None, :, None]) & (reached.T[:, None, :] == 1)
    selection = picked.reshape(nodes * capacity, count_tok).astype(jnp.bfloat16)
    send_rows = (
        jnp.dot(selection, tokens, preferred_element_type=jnp.float32)
        .astype(jnp.bfloat16)
        .reshape(nodes, capacity, width)
    )
    expert_labels = jnp.arange(nodes * EXP_NODE, dtype=jnp.int32)
    matches = expert_ids[:, :, None] == expert_labels[None, None, :]
    gate_table = jnp.sum(
        jnp.where(matches, gate_values.astype(jnp.float32)[:, :, None], jnp.float32(0.0)), axis=1
    )
    gate_table = gate_table.reshape(count_tok, nodes, EXP_NODE)
    slot_gates = jnp.einsum("mct,tmk->mck", picked.astype(jnp.float32), gate_table).astype(
        jnp.bfloat16
    )
    arrived, arrived_gates = (
        lax.all_to_all(send_rows, "node", split_axis=0, concat_axis=0, tiled=True),
        lax.all_to_all(slot_gates, "node", split_axis=0, concat_axis=0, tiled=True),
    )
    gathered, gathered_gates = (
        lax.all_gather(arrived, "local", axis=0, tiled=True),
        lax.all_gather(arrived_gates, "local", axis=0, tiled=True),
    )
    rows_all = gathered.reshape(-1, width)
    gates_all = gathered_gates.reshape(-1, EXP_NODE)
    which = lax.axis_index("local") // split
    own_gate = lax.dynamic_slice_in_dim(gates_all, which, 1, 1).astype(jnp.float32)
    gate = jnp.dot(rows_all, w_gate[0], preferred_element_type=jnp.float32)
    upper = jnp.dot(rows_all, w_up[0], preferred_element_type=jnp.float32)
    gated = (own_gate * jax.nn.silu(gate) * upper).astype(jnp.bfloat16)
    down_w = w_down[0]
    own_rows = lax.psum_scatter(
        jnp.dot(gated, down_w, preferred_element_type=jnp.float32).astype(jnp.bfloat16),
        "local",
        scatter_dimension=0,
        tiled=True,
    )
    returned = lax.all_to_all(
        own_rows.reshape(nodes, capacity, width), "node", split_axis=0, concat_axis=0, tiled=True
    )
    mixed = jnp.dot(
        selection.T, returned.reshape(nodes * capacity, width), preferred_element_type=jnp.float32
    )
    return mixed.astype(jnp.bfloat16)


def solution(mesh):
    placed = (
        P(("rep", "node", "local"), None),
        P(("rep", "node", "local"), None),
        P(("rep", "node", "local"), None),
        P(("node", "local"), None, None),
        P(("node", "local"), None, None),
        P(("node", "local"), None, None),
    )
    paired = mesh.shape["node"] == 4 and mesh.shape["local"] == 4
    return jax.shard_map(
        fused if paired else local,
        mesh=mesh,
        in_specs=placed,
        out_specs=P(("rep", "node", "local"), None),
        check_vma=False,
    )
```

```python
import functools

import jax
import jax.numpy as jnp
from jax import lax
from jax.experimental import pallas as pl
from jax.experimental.pallas import tpu as pltpu
from jax.sharding import PartitionSpec as P

EXP_NODE = 2
MESH = pl.DeviceIdType.MESH
F32 = jnp.float32
BF16 = jnp.bfloat16
LANES = 128
GATE_TILE = 256
TILE = 512
NT = (((1,), (1,)), ((), ()))

TOK, TBL, OUT, Z, Y, C1, C2, RC, RY, RZ = 0, 1, 2, 4, 12, 20, 24, 28, 32, 40
SEMS = 48
SLOT = (1, 3, 2, 0)


def fused_kernel(
    cap,
    tokens,
    ids_t,
    gates_t,
    w_gate,
    w_up,
    w_down,
    out,
    wg,
    wu,
    wd,
    x,
    sendz,
    tok_n,
    tbl,
    rows_before,
    rows_reached,
    sel,
    hid,
    crecv,
    yrecv,
    zret,
    load_sem,
    send_sem,
    recv_sem,
):
    half = tokens.shape[1] // 2
    count_tok = tokens.shape[0]
    pair = 2 * cap
    ff = wg.shape[1]
    me = lax.axis_index("node")
    lane = lax.axis_index("local")
    y = lane // 2
    c = lane % 2
    core_nbr = {"local": lane + 1 - 2 * c}
    y_nbr = {"local": (lane + 2) % 4}
    node_of = [me, me + 1 - 2 * (me % 2), (me + 2) % 4, 3 - me]

    loads = [
        pltpu.make_async_copy(src.at[0], dst, load_sem.at[i])
        for i, (src, dst) in enumerate(((w_gate, wg), (w_up, wu), (w_down, wd)))
    ]
    barrier = pltpu.get_barrier_semaphore()
    partners = [core_nbr, y_nbr] + [{"node": node_of[k]} for k in (1, 2, 3)]
    for partner in partners:
        pl.semaphore_signal(barrier, inc=1, device_id=partner, device_id_type=MESH)
    pl.semaphore_wait(barrier, len(partners))

    def remote(src, dst, number, device):
        return pltpu.make_async_remote_copy(
            src_ref=src,
            dst_ref=dst,
            send_sem=send_sem.at[number],
            recv_sem=recv_sem.at[number],
            device_id=device,
            device_id_type=MESH,
        )

    own_at = pl.multiple_of(c * half, LANES)
    nbr_at = pl.multiple_of((1 - c) * half, LANES)
    tok_copy = remote(tokens.at[:, pl.ds(nbr_at, half)], tok_n, TOK, core_nbr)
    tok_copy.start()
    row = lax.broadcasted_iota(jnp.int32, (LANES, count_tok), 0)
    tbl[0] = jnp.where(ids_t[0:1, :] == row, gates_t[0:1, :], 0.0) + jnp.where(
        ids_t[1:2, :] == row, gates_t[1:2, :], 0.0
    )
    tbl_copy = remote(tbl.at[0], tbl.at[1], TBL, core_nbr)
    tbl_copy.start()

    def select(which, first):
        named = jnp.where(tbl[which] != 0.0, 1.0, 0.0).astype(BF16)
        pool = jnp.where(
            lax.broadcasted_iota(jnp.int32, (8, LANES), 1) // EXP_NODE
            == lax.broadcasted_iota(jnp.int32, (8, LANES), 0),
            1.0,
            0.0,
        ).astype(BF16)
        reached = jnp.minimum(jnp.dot(pool, named, preferred_element_type=F32), 1.0)
        upper = jnp.where(
            lax.broadcasted_iota(jnp.int32, (count_tok, count_tok), 0)
            < lax.broadcasted_iota(jnp.int32, (count_tok, count_tok), 1),
            1.0,
            0.0,
        ).astype(BF16)
        rows_before[...] = jnp.dot(reached.astype(BF16), upper, preferred_element_type=F32)
        rows_reached[...] = reached
        slot = lax.broadcasted_iota(jnp.int32, (pair, count_tok), 0)
        for k in range(4):
            before = rows_before[pl.ds(node_of[k], 1), :].astype(jnp.int32) + first
            there = rows_reached[pl.ds(node_of[k], 1), :]
            sel[which, k * pair : (k + 1) * pair, :] = jnp.where(
                before == slot, there, 0.0
            ).astype(BF16)

    select(0, cap * c)
    tbl_copy.wait_recv()
    select(1, cap * (1 - c))
    tok_copy.wait_recv()

    def build(k, dst):
        s_own = sel[0, k * pair : (k + 1) * pair, :]
        s_nbr = sel[1, k * pair : (k + 1) * pair, :]
        gates = lax.dot_general(
            s_own, tbl[0].astype(BF16), NT, preferred_element_type=F32
        ) + lax.dot_general(s_nbr, tbl[1].astype(BF16), NT, preferred_element_type=F32)
        dst[:, half : half + LANES] = gates.astype(BF16)

        @pl.loop(0, half // TILE)
        def _(j):
            at = pl.multiple_of(j * TILE, TILE)
            here = pl.multiple_of(own_at + at, LANES)
            got = jnp.dot(s_own, tokens[:, pl.ds(here, TILE)], preferred_element_type=F32)
            got += jnp.dot(s_nbr, tok_n[:, pl.ds(at, TILE)], preferred_element_type=F32)
            dst[:, pl.ds(at, TILE)] = got.astype(BF16)

    cut = half // 2
    going = (pl.ds(0, cut), pl.ds(cut, half - cut + LANES))
    coming = (pl.ds(0, cut), pl.ds(cut, half - cut))

    def z_copy(k, p):
        return remote(
            sendz.at[k - 1, :, going[p]],
            x.at[c, SLOT[k], y, :, going[p]],
            Z + 2 * k + p,
            {"node": node_of[k]},
        )

    def y_copy(k, p):
        here = x.at[c, SLOT[k], y, :, going[p]]
        return remote(here, here, Y + 2 * k + p, y_nbr)

    def c1_copy(k):
        here = x.at[c, SLOT[k], y]
        return remote(here, here, C1 + k, core_nbr)

    def c2_copy(k):
        here = x.at[c, SLOT[k], 1 - y]
        return remote(here, here, C2 + k, core_nbr)

    def rc_copy(k):
        return remote(
            x.at[1 - c, SLOT[k], :, :, pl.ds(0, half)], crecv.at[k], RC + k, core_nbr
        )

    def ry_copy(k, p):
        return remote(
            crecv.at[k, 1 - y, :, coming[p]], yrecv.at[k, :, coming[p]], RY + 2 * k + p, y_nbr
        )

    def rz_copy(k, p):
        return remote(
            crecv.at[k, y, :, coming[p]],
            zret.at[k, :, coming[p]],
            RZ + 2 * k + p,
            {"node": node_of[k]},
        )

    def take_z(k, p):
        if k > 0:
            z_copy(k, p).wait_recv()
        y_copy(k, p).start()
        if p == 1:
            c1_copy(k).start()

    def take_y(k):
        for p in range(2):
            y_copy(k, p).wait_recv()
        c2_copy(k).start()

    count = 2 * 2 * pair

    def up(rounds):
        first = SLOT[rounds[0]]
        both = pl.ds(first, 2)
        for k in rounds:
            c1_copy(k).wait_recv()
            c2_copy(k).wait_recv()
        table = x[c, both, :, :, half : half + LANES].reshape(count, LANES).astype(F32)
        mine = lax.broadcasted_iota(jnp.int32, (count, LANES), 1) == me * EXP_NODE + y
        weight = jnp.sum(jnp.where(mine, table, 0.0), axis=1, keepdims=True)

        @pl.loop(0, ff // GATE_TILE)
        def _(j):
            cols = pl.ds(pl.multiple_of(j * GATE_TILE, GATE_TILE), GATE_TILE)
            x0 = x[0, both, :, :, :half].reshape(count, half)
            x1 = x[1, both, :, :, :half].reshape(count, half)
            gate = jnp.dot(x0, wg[:half, cols], preferred_element_type=F32)
            gate += jnp.dot(x1, wg[half:, cols], preferred_element_type=F32)
            upper = jnp.dot(x0, wu[:half, cols], preferred_element_type=F32)
            upper += jnp.dot(x1, wu[half:, cols], preferred_element_type=F32)
            hid[:, cols] = (weight * (gate / (1.0 + jnp.exp(-gate))) * upper).astype(BF16)

    def down(rounds, h):
        both = pl.ds(SLOT[rounds[0]], 2)

        @pl.loop(0, half // TILE)
        def _(j):
            at = pl.multiple_of(j * TILE, TILE)
            part = jnp.dot(
                hid[...],
                wd[:, pl.ds(pl.multiple_of(h * half + at, TILE), TILE)],
                preferred_element_type=F32,
            )
            x[h, both, :, :, pl.ds(at, TILE)] = part.astype(BF16).reshape(2, 2, pair, TILE)

    def down_nbr(rounds):
        down(rounds, 1 - c)
        for k in rounds:
            rc_copy(k).start()

    def down_own(rounds):
        for k in rounds:
            c1_copy(k).wait_send()
            c2_copy(k).wait_send()
            for p in range(2):
                y_copy(k, p).wait_send()
        down(rounds, c)

    def fold_core(k):
        rc_copy(k).wait_recv()
        for p in range(2):
            cols = coming[p]
            crecv[k, 1 - y, :, cols] = (
                crecv[k, 1 - y, :, cols].astype(F32)
                + x[c, SLOT[k], 1 - y, :, cols].astype(F32)
            ).astype(BF16)
            ry_copy(k, p).start()

    def fold_y(k):
        for p in range(2):
            cols = coming[p]
            ry_copy(k, p).wait_recv()
            total = (
                crecv[k, y, :, cols].astype(F32)
                + x[c, SLOT[k], y, :, cols].astype(F32)
                + yrecv[k, :, cols].astype(F32)
            ).astype(BF16)
            if k == 0:
                zret[0, :, cols] = total
            else:
                crecv[k, y, :, cols] = total
                rz_copy(k, p).start()

    build(3, sendz.at[2])
    z_copy(3, 0).start()
    z_copy(3, 1).start()
    build(1, sendz.at[0])
    z_copy(1, 0).start()
    z_copy(1, 1).start()
    build(0, x.at[c, SLOT[0], y])
    take_z(0, 0)
    take_z(0, 1)
    for load in loads:
        load.start()
    build(2, sendz.at[1])
    take_z(3, 0)
    z_copy(3, 0).wait_send()
    z_copy(2, 0).start()
    take_y(0)
    take_z(3, 1)
    z_copy(3, 1).wait_send()
    z_copy(2, 1).start()
    take_z(1, 0)
    take_z(1, 1)
    take_y(3)
    for load in loads:
        load.wait()
    up((3, 0))
    take_y(1)
    take_z(2, 0)
    down_nbr((3, 0))
    take_z(2, 1)
    down_own((3, 0))
    fold_core(3)
    take_y(2)
    fold_y(3)
    fold_core(0)
    up((2, 1))
    down_nbr((2, 1))
    down_own((2, 1))
    fold_core(2)
    for p in range(2):
        ry_copy(2, p).wait_send()
    fold_core(1)
    fold_y(0)
    fold_y(2)
    fold_y(1)

    eye = jnp.where(
        lax.broadcasted_iota(jnp.int32, (count_tok, count_tok), 0)
        == lax.broadcasted_iota(jnp.int32, (count_tok, count_tok), 1),
        1.0,
        0.0,
    ).astype(BF16)
    for k in (1, 2, 3):
        for p in range(2):
            rz_copy(k, p).wait_recv()
    out_copy = remote(
        tok_n, out.at[:, pl.ds(own_at, half)], OUT, core_nbr
    )
    for which in (1, 0):
        back = lax.dot_general(eye, sel[which], NT, preferred_element_type=F32).astype(BF16)

        @pl.loop(0, half // TILE)
        def _(j):
            at = pl.multiple_of(j * TILE, TILE)
            got = zret[:, :, pl.ds(at, TILE)].reshape(4 * pair, TILE)
            mixed = jnp.dot(back, got, preferred_element_type=F32).astype(BF16)
            if which == 1:
                tok_n[:, pl.ds(at, TILE)] = mixed
            else:
                out[:, pl.ds(pl.multiple_of(own_at + at, LANES), TILE)] = mixed

        if which == 1:
            out_copy.start()
    out_copy.wait()
    tok_copy.wait_send()
    tbl_copy.wait_send()
    for p in range(2):
        z_copy(1, p).wait_send()
        z_copy(2, p).wait_send()
    for k in range(4):
        rc_copy(k).wait_send()
        for p in range(2):
            if k != 2:
                ry_copy(k, p).wait_send()
            if k > 0:
                rz_copy(k, p).wait_send()


def fused(tokens, expert_ids, gate_values, w_gate, w_up, w_down):
    count_tok, width = tokens.shape
    nodes = lax.axis_size("node")
    cap = 3 * count_tok // (2 * nodes)
    pair = 2 * cap
    half = width // 2
    ff = w_gate.shape[2]
    vmem = pl.BlockSpec(memory_space=pltpu.VMEM)
    hbm = pl.BlockSpec(memory_space=pl.ANY)
    dma = pltpu.SemaphoreType.DMA
    return pl.pallas_call(
        functools.partial(fused_kernel, cap),
        out_shape=jax.ShapeDtypeStruct((count_tok, width), BF16),
        in_specs=[vmem, vmem, vmem, hbm, hbm, hbm],
        out_specs=vmem,
        scratch_shapes=[
            pltpu.VMEM((width, ff), BF16),
            pltpu.VMEM((width, ff), BF16),
            pltpu.VMEM((ff, width), BF16),
            pltpu.VMEM((2, nodes, 2, pair, half + LANES), BF16),
            pltpu.VMEM((nodes - 1, pair, half + LANES), BF16),
            pltpu.VMEM((count_tok, half), BF16),
            pltpu.VMEM((2, LANES, count_tok), F32),
            pltpu.VMEM((8, count_tok), F32),
            pltpu.VMEM((8, count_tok), F32),
            pltpu.VMEM((2, nodes * pair, count_tok), BF16),
            pltpu.VMEM((4 * pair, ff), BF16),
            pltpu.VMEM((nodes, 2, pair, half), BF16),
            pltpu.VMEM((nodes, pair, half), BF16),
            pltpu.VMEM((nodes, pair, half), BF16),
            dma((3,)),
            dma((SEMS,)),
            dma((SEMS,)),
        ],
        compiler_params=pltpu.CompilerParams(
            collective_id=0, has_side_effects=True, vmem_limit_bytes=61 * 1024 * 1024
        ),
        cost_estimate=pl.CostEstimate(
            flops=12 * nodes * pair * width * ff,
            bytes_accessed=6 * width * ff,
            transcendentals=2 * nodes * pair * ff,
        ),
    )(
        tokens,
        expert_ids.T,
        gate_values.astype(F32).T,
        w_gate,
        w_up,
        w_down,
    )


def local(tokens, expert_ids, gate_values, w_gate, w_up, w_down):
    nodes = lax.axis_size("node")
    lanes = lax.axis_size("local")
    split = lanes // EXP_NODE
    width = tokens.shape[1]
    count_tok = tokens.shape[0]
    capacity = 3 * count_tok // (2 * nodes)
    node_labels = jnp.arange(nodes, dtype=jnp.int32)
    owner = expert_ids // EXP_NODE
    reached = jnp.any(owner[:, :, None] == node_labels[None, None, :], axis=1).astype(jnp.int32)
    before = jnp.cumsum(reached, axis=0) - reached
    slot_labels = jnp.arange(capacity, dtype=jnp.int32)
    picked = (before.T[:, None, :] == slot_labels[None, :, None]) & (reached.T[:, None, :] == 1)
    selection = picked.reshape(nodes * capacity, count_tok).astype(jnp.bfloat16)
    send_rows = (
        jnp.dot(selection, tokens, preferred_element_type=jnp.float32)
        .astype(jnp.bfloat16)
        .reshape(nodes, capacity, width)
    )
    expert_labels = jnp.arange(nodes * EXP_NODE, dtype=jnp.int32)
    matches = expert_ids[:, :, None] == expert_labels[None, None, :]
    gate_table = jnp.sum(
        jnp.where(matches, gate_values.astype(jnp.float32)[:, :, None], jnp.float32(0.0)), axis=1
    )
    gate_table = gate_table.reshape(count_tok, nodes, EXP_NODE)
    slot_gates = jnp.einsum("mct,tmk->mck", picked.astype(jnp.float32), gate_table).astype(
        jnp.bfloat16
    )
    arrived, arrived_gates = (
        lax.all_to_all(send_rows, "node", split_axis=0, concat_axis=0, tiled=True),
        lax.all_to_all(slot_gates, "node", split_axis=0, concat_axis=0, tiled=True),
    )
    gathered, gathered_gates = (
        lax.all_gather(arrived, "local", axis=0, tiled=True),
        lax.all_gather(arrived_gates, "local", axis=0, tiled=True),
    )
    rows_all = gathered.reshape(-1, width)
    gates_all = gathered_gates.reshape(-1, EXP_NODE)
    which = lax.axis_index("local") // split
    own_gate = lax.dynamic_slice_in_dim(gates_all, which, 1, 1).astype(jnp.float32)
    gate = jnp.dot(rows_all, w_gate[0], preferred_element_type=jnp.float32)
    upper = jnp.dot(rows_all, w_up[0], preferred_element_type=jnp.float32)
    gated = (own_gate * jax.nn.silu(gate) * upper).astype(jnp.bfloat16)
    down_w = w_down[0]
    own_rows = lax.psum_scatter(
        jnp.dot(gated, down_w, preferred_element_type=jnp.float32).astype(jnp.bfloat16),
        "local",
        scatter_dimension=0,
        tiled=True,
    )
    returned = lax.all_to_all(
        own_rows.reshape(nodes, capacity, width), "node", split_axis=0, concat_axis=0, tiled=True
    )
    mixed = jnp.dot(
        selection.T, returned.reshape(nodes * capacity, width), preferred_element_type=jnp.float32
    )
    return mixed.astype(jnp.bfloat16)


def solution(mesh):
    placed = (
        P(("rep", "node", "local"), None),
        P(("rep", "node", "local"), None),
        P(("rep", "node", "local"), None),
        P(("node", "local"), None, None),
        P(("node", "local"), None, None),
        P(("node", "local"), None, None),
    )
    paired = mesh.shape["node"] == 4 and mesh.shape["local"] == 4
    return jax.shard_map(
        fused if paired else local,
        mesh=mesh,
        in_specs=placed,
        out_specs=P(("rep", "node", "local"), None),
        check_vma=False,
    )
```
